256 devices in a mesh: row: 16 (over x_lo, z), col: 16 (over y, x_hi, core).
Axes of the slice: x: 4 (x_hi: 2, x_lo: 2; x = x_hi * 2 + x_lo), y: 4, z: 8, core: 2. Of those that a mesh axis runs over, the one named last changes fastest.
Arguments:
- tokens: bfloat16 [1024, 8192], P('col', 'row'), may hold values from -6 to 6
- up_weight: bfloat16 [8192, 28672], P('row', 'col'), may hold values from -0.0625 to 0.0625
- down_weight: bfloat16 [28672, 8192], P('col', 'row'), may hold values from -0.03125 to 0.03125
- output_grad: bfloat16 [1024, 8192], P('col', 'row'), may hold values from -1.5 to 1.5
Outputs:
- output: bfloat16 [1024, 8192], P('col', 'row')
- input_grad: bfloat16 [1024, 8192], P('col', 'row')
- up_grad: bfloat16 [8192, 28672], P('row', 'col')
- down_grad: bfloat16 [28672, 8192], P('col', 'row')
The draws below stay inside these ranges and needn't reach their ends.
All inputs are finite; a program needn't handle non-finite values.
Results may differ from the reference program's by a relative error of at most 0.005.
Values may be sent and summed in bfloat16 or wider, within the bound.
No kernel may reach another device: no remote copies, remote signals or barrier semaphores. Data moves between devices by JAX's collectives and lax.ppermute only.
A program may use at most 128 MiB of HBM per device.

```python
import jax
import jax.numpy as jnp

D = 8192
FF = 28672
TOKENS = 1024


def with_spikes(result, own_key, source, target, blocks, factor):
    def block_of(axis_at):
        return (jnp.arange(result.shape[axis_at]) // (result.shape[axis_at] // blocks)).reshape((-1,) + (1,) * (result.ndim - 1 - axis_at))

    near = jax.random.permutation(own_key, blocks)[block_of(target)]
    second = (block_of(target) + blocks // 2) % blocks
    return jnp.where((block_of(source) == near) | (block_of(source) == second), factor * result, result)


def block_levels(rng, extent, pieces, low, top_value):
    def one(axis_at, parts):
        draws = jax.random.uniform(jax.random.fold_in(jax.random.fold_in(rng, 6), axis_at), (parts,), jnp.float32, low / len(pieces), top_value / len(pieces))
        return jnp.repeat(jnp.exp(draws), extent[axis_at] // parts).reshape((-1,) + (1,) * (len(extent) - axis_at - 1))

    gain = one(*pieces[0])
    for cut in pieces[1:]:
        gain = gain * one(*cut)
    return gain


def bell_draw(own_key, shape, width, limit, split=(), dtype=jnp.bfloat16):
    loudness = block_levels(own_key, shape, split, -0.22, 0.18) if split else 1.0
    result = jax.random.normal(own_key, shape, jnp.float32) * width * loudness
    return jnp.minimum(jnp.maximum(result, -limit), limit).astype(dtype)


def noise_with(key, shape, spread, reach, split, heavy, held_as=jnp.bfloat16):
    values = spread * jax.random.normal(key, shape, jnp.float32)
    if split:
        values = values * block_levels(key, shape, split, -0.22, 0.18)
    return jnp.clip(with_spikes(values, jax.random.fold_in(key, 3), *heavy), -reach, reach).astype(held_as)


def setup_inputs(seed: int = 0) -> dict:
    key_list = jax.random.split(jax.random.key(seed), 5)
    tokens = noise_with(key_list[0], (TOKENS, D), 1.0, 6.0, ((0, 16), (1, 16)), (1, 0, 16, 2.0))
    up_weight = bell_draw(key_list[1], (D, FF), D ** -0.5, 0.0625, ((0, 16), (1, 16)))
    down_weight = bell_draw(key_list[2], (FF, D), FF ** -0.5, 0.03125, ((0, 16), (1, 16)))
    output_grad = noise_with(key_list[3], (TOKENS, D), 0.25, 1.5, ((0, 16), (1, 16)), (1, 0, 16, 2.0))
    return dict(tokens=tokens, up_weight=up_weight, down_weight=down_weight, output_grad=output_grad)


gelu_scale = 0.7978845608028654

def gelu_tanh(values):
    return 0.5 * values * (1.0 + jnp.tanh(gelu_scale * (values + 0.044715 * values * values * values)))

def reference(tokens, up_weight, down_weight, output_grad):
    pre = jnp.dot(tokens, up_weight, preferred_element_type=jnp.float32)
    activ, pullback = jax.vjp(gelu_tanh, pre)
    hidden = activ.astype(jnp.bfloat16)
    output = jnp.dot(hidden, down_weight, preferred_element_type=jnp.float32).astype(jnp.bfloat16)
    hidden_grad = jnp.dot(output_grad, down_weight.T, preferred_element_type=jnp.float32)
    pre_grad = pullback(hidden_grad)[0].astype(jnp.bfloat16)
    input_grad = jnp.dot(pre_grad, up_weight.T, preferred_element_type=jnp.float32).astype(jnp.bfloat16)
    up_grad = jnp.dot(tokens.T, pre_grad, preferred_element_type=jnp.float32).astype(jnp.bfloat16)
    down_grad = jnp.dot(hidden.T, output_grad, preferred_element_type=jnp.float32).astype(jnp.bfloat16)
    return (output, input_grad, up_grad, down_grad)
```

```python
import jax
import jax.numpy as jnp
from jax import lax
from jax.sharding import Mesh
from jax.sharding import PartitionSpec as P

gelu_scale = 0.7978845608028654
wide, thin = jnp.float32, jnp.bfloat16


def gelu_tanh(values):
    return (
        0.5 * values * (1.0 + jnp.tanh(gelu_scale * (values + 0.044715 * values * values * values)))
    )


def dot(left, right, left_dim, right_dim):
    return lax.dot_general(
        left, right, (((left_dim,), (right_dim,)), ((), ())), preferred_element_type=wide
    )


def shift(block, axis, by):
    size = lax.axis_size(axis)
    return lax.ppermute(block, axis, [(at, (at + by) % size) for at in range(size)])


def ring_sum(part, axis, way):
    half = lax.axis_size(axis) // 2
    ahead, behind = part(way * half).astype(thin), None
    for step in range(1, half + 1):
        ahead = shift(ahead, axis, way).astype(wide)
        if step > 1:
            behind = shift(behind, axis, -way).astype(wide)
        if step < half:
            ahead = (part(way * (half - step)) + ahead).astype(thin)
            term = part(-way * (half - step))
            behind = (term if behind is None else term + behind).astype(thin)
    return part(0) + ahead + behind


def ring_spread(block, axis, way, put):
    half = lax.axis_size(axis) // 2
    put(0, block)
    ahead = behind = block
    for step in range(1, half + 1):
        ahead = shift(ahead, axis, way)
        put(-way * step, ahead)
        if step < half:
            behind = shift(behind, axis, -way)
            put(way * step, behind)


def gather_col(block):
    block = jnp.concatenate([block, shift(block, "xh", 1)], axis=0)
    block = jnp.concatenate(
        [block, shift(block, "y", -1), shift(block, "y", 1), shift(block, "y", 2)], axis=0
    )
    return jnp.concatenate([block, shift(block, "core", 1)], axis=0)


def scatter_col(total):
    half = total.shape[0] // 2
    total = total[:half] + shift(total[half:], "core", 1)
    own, after, before, across = jnp.split(total, 4, axis=0)
    own = (
        own
        + shift(after.astype(thin), "y", 1).astype(wide)
        + shift(before.astype(thin), "y", -1).astype(wide)
        + shift(across.astype(thin), "y", 2).astype(wide)
    )
    half = own.shape[0] // 2
    return (own[:half] + shift(own[half:], "xh", 1)).astype(thin)


def local(tokens, up_weight, down_weight, output_grad):
    width = tokens.shape[1]
    hidden_width = up_weight.shape[1]
    panel = gather_col(jnp.concatenate([tokens, output_grad], axis=1))
    tok_panel, grad_panel = panel[:, :width], panel[:, width:]
    count = panel.shape[0]
    spots = lax.axis_size("z")
    share = count // (2 * spots)
    here, side = lax.axis_index("z"), lax.axis_index("xl")

    def half_of(which):
        return lax.dynamic_slice_in_dim(tok_panel, which * (count // 2), count // 2, 0)

    pre_sent = dot(half_of(1 - side), up_weight, 1, 0).astype(thin)
    pre_half = dot(half_of(side), up_weight, 1, 0) + shift(pre_sent, "xl", 1).astype(wide)

    def pre_part(away):
        return lax.dynamic_slice_in_dim(pre_half, (here + away) % spots * share, share, 0)

    pre_own = ring_sum(pre_part, "z", 1)

    grad_view = grad_panel.reshape(2, spots, share, width)

    def grad_part(away):
        rows = lax.dynamic_slice_in_dim(grad_view, (here + away) % spots, 1, 1)
        return dot(rows.reshape(2 * share, width), down_weight, 1, 1)

    grad_two = ring_sum(grad_part, "z", -1)
    grad_mine = lax.dynamic_slice_in_dim(grad_two, side * share, share, 0)
    grad_other = lax.dynamic_slice_in_dim(grad_two, (1 - side) * share, share, 0)
    grad_own = grad_mine + shift(grad_other.astype(thin), "xl", 1).astype(wide)

    activ_own, pullback = jax.vjp(gelu_tanh, pre_own)
    activ_own = activ_own.astype(thin)
    slope_own = pullback(grad_own)[0].astype(thin)

    act_half = [jnp.zeros((count // 2, hidden_width), thin)]

    def put_act(away, value):
        act_half[0] = lax.dynamic_update_slice_in_dim(
            act_half[0], value, (here + away) % spots * share, 0
        )

    ring_spread(activ_own, "z", 1, put_act)
    act_far = shift(act_half[0], "xl", 1)
    act_panel = jnp.concatenate(
        [jnp.where(side == 0, act_half[0], act_far), jnp.where(side == 0, act_far, act_half[0])],
        axis=0,
    )

    slope_far = shift(slope_own, "xl", 1)
    slope_two = jnp.stack(
        [jnp.where(side == 0, slope_own, slope_far), jnp.where(side == 0, slope_far, slope_own)]
    )[:, None]
    slope_view = [jnp.zeros((2, spots, share, hidden_width), thin)]

    def put_slope(away, value):
        slope_view[0] = lax.dynamic_update_slice_in_dim(
            slope_view[0], value, (here + away) % spots, 1
        )

    ring_spread(slope_two, "z", -1, put_slope)
    slope_panel = slope_view[0].reshape(count, hidden_width)

    output = scatter_col(dot(act_panel, down_weight, 1, 0))
    down_grad = dot(act_panel, grad_panel, 0, 0).astype(thin)
    input_grad = scatter_col(dot(slope_panel, up_weight, 1, 1))
    up_grad = dot(tok_panel, slope_panel, 0, 0).astype(thin)
    return (output, input_grad, up_grad, down_grad)


def solution(mesh):
    fine = Mesh(mesh.devices.reshape(2, 8, 4, 2, 2), ("xl", "z", "y", "xh", "core"))
    row, col = ("xl", "z"), ("y", "xh", "core")
    placed = (P(col, row), P(row, col), P(col, row), P(col, row))
    return jax.shard_map(
        local,
        mesh=fine,
        in_specs=placed,
        out_specs=(P(col, row), P(col, row), P(row, col), P(col, row)),
        check_vma=False,
    )
```

```python
import jax
import jax.numpy as jnp
from jax import lax
from jax.sharding import Mesh
from jax.sharding import PartitionSpec as P

gelu_scale = 0.7978845608028654
wide, thin = jnp.float32, jnp.bfloat16


def gelu_tanh(values):
    return (
        0.5 * values * (1.0 + jnp.tanh(gelu_scale * (values + 0.044715 * values * values * values)))
    )


def dot(left, right, left_dim, right_dim):
    return lax.dot_general(
        left, right, (((left_dim,), (right_dim,)), ((), ())), preferred_element_type=wide
    )


def shift(block, axis, by):
    size = lax.axis_size(axis)
    return lax.ppermute(block, axis, [(at, (at + by) % size) for at in range(size)])


def ring_sum(part, axis, way):
    half = lax.axis_size(axis) // 2
    ahead, behind = part(way * half).astype(thin), None
    for step in range(1, half + 1):
        ahead = shift(ahead, axis, way).astype(wide)
        if step > 1:
            behind = shift(behind, axis, -way).astype(wide)
        if step < half:
            ahead = (part(way * (half - step)) + ahead).astype(thin)
            term = part(-way * (half - step))
            behind = (term if behind is None else term + behind).astype(thin)
    return part(0) + ahead + behind


def ring_spread(block, axis, way, put, hooks=None):
    half = lax.axis_size(axis) // 2
    put(0, block)
    ahead = behind = block
    for step in range(1, half + 1):
        if hooks and step in hooks:
            ahead = hooks[step](ahead)
        ahead = shift(ahead, axis, way)
        put(-way * step, ahead)
        if step < half:
            behind = shift(behind, axis, -way)
            put(way * step, behind)


def send_to(block, axes, where):
    sizes = [lax.axis_size(axis) for axis in axes]
    total = 1
    for size in sizes:
        total *= size

    def target(at):
        spots, rest = [], at
        for size in reversed(sizes):
            spots.append(rest % size)
            rest //= size
        index = 0
        for spot, size, by in zip(reversed(spots), sizes, where):
            index = index * size + (spot + by) % size
        return index

    return lax.ppermute(block, axes, [(at, target(at)) for at in range(total)])


def gather_first(block):
    side = shift(block, "xl", 1)
    below = shift(block, "xh", 1)
    corner = send_to(block, ("xl", "xh"), (1, 1))
    return jnp.concatenate(
        [
            jnp.concatenate([block, side], axis=1),
            jnp.concatenate([below, corner], axis=1),
        ],
        axis=0,
    )


def gather_y(block):
    return [block, shift(block, "y", -1), shift(block, "y", 1), shift(block, "y", 2)]


def gather_core(blocks):
    block = jnp.concatenate(blocks, axis=0)
    return jnp.concatenate([block, shift(block, "core", 1)], axis=0)


def tie(*values):
    return lax.optimization_barrier(values)


def after(value, *others):
    return lax.optimization_barrier((value, *others))[0]


def sum_core(rows, near, far, near_dim):
    half = rows.shape[0] // 2
    other, own = rows[half:], rows[:half]
    far_got = shift(dot(other, far, 1, near_dim), "core", 1)
    near_got = shift(dot(other, near, 1, near_dim), "core", 1)
    far_sum = dot(own, far, 1, near_dim) + far_got
    near_sum = dot(own, near, 1, near_dim) + near_got
    return jnp.concatenate([near_sum, far_sum], axis=1)


def cut_y(total):
    mine, following, before, across = jnp.split(total, 4, axis=0)
    return mine, following.astype(thin), before.astype(thin), across.astype(thin)


def sum_y(mine, following, before, across):
    return (
        mine
        + shift(following, "y", 1).astype(wide)
        + shift(before, "y", -1).astype(wide)
        + shift(across, "y", 2).astype(wide)
    )


def sum_x(mine):
    rows, columns = mine.shape[0] // 2, mine.shape[1] // 2
    return (
        shift(mine[:rows, columns:], "xl", 1),
        shift(mine[rows:, :columns], "xh", 1),
        send_to(mine[rows:, columns:], ("xl", "xh"), (1, 1)),
        mine[:rows, :columns],
    )


def local(tokens, up_weight, down_weight, output_grad):
    width = tokens.shape[1]
    part_width = up_weight.shape[1] // 2
    spots = lax.axis_size("z")
    here, side = lax.axis_index("z"), lax.axis_index("xl")

    def up_cut(which):
        return lax.dynamic_slice_in_dim(up_weight, which * part_width, part_width, 1)

    def down_cut(which):
        return lax.dynamic_slice_in_dim(down_weight, which * part_width, part_width, 0)

    both = gather_first(jnp.concatenate([tokens, output_grad], axis=0))
    both = both.reshape(2, 2, tokens.shape[0], 2 * width)
    tok_first = both[:, 0].reshape(-1, 2 * width)
    grad_first = both[:, 1].reshape(-1, 2 * width)
    up_sent, tok_first = tie(up_cut(1 - side), tok_first)
    up_far = shift(up_sent, "xl", 1)
    down_cut_far, up_far = tie(down_cut(1 - side), up_far)
    down_far = shift(down_cut_far, "xl", 1)
    tok_blocks = gather_y(tok_first)
    tok_panel = gather_core(tok_blocks)
    grad_blocks = gather_y(after(grad_first, *tok_blocks))
    grad_panel = gather_core(grad_blocks)
    up_near, down_near = up_cut(side), down_cut(side)
    count = tok_panel.shape[0]
    share = count // spots

    pre_near = dot(tok_panel[:, :width], up_near, 1, 0)
    pre_part = pre_near + dot(tok_panel[:, width:], up_far, 1, 0)
    grad_near = dot(grad_panel[:, :width], down_near, 1, 1)
    grad_part = grad_near + dot(grad_panel[:, width:], down_far, 1, 1)

    def rows_of(panel, away):
        return lax.dynamic_slice_in_dim(panel, (here + away) % spots * share, share, 0)

    pre_own = ring_sum(lambda away: rows_of(pre_part, away), "z", 1)
    grad_own = ring_sum(lambda away: rows_of(grad_part, away), "z", -1)

    activ_own, pullback = jax.vjp(gelu_tanh, pre_own)
    activ_own = activ_own.astype(thin)
    slope_own = pullback(grad_own)[0].astype(thin)

    def spread(block, way, hooks=None):
        panel = [jnp.zeros((count, part_width), thin)]

        def put(away, value):
            panel[0] = lax.dynamic_update_slice_in_dim(
                panel[0], value, (here + away) % spots * share, 0
            )

        ring_spread(block, "z", way, put, hooks)
        return panel[0]

    def put_half(whole, value, which, axis):
        return lax.dynamic_update_slice_in_dim(whole, value, which * part_width, axis)

    act_panel = spread(activ_own, 1)
    down_prod = dot(act_panel, grad_panel[:, width:], 0, 0).astype(thin)
    down_sent = shift(down_prod, "xl", 1)
    out_cut = list(cut_y(sum_core(act_panel, down_near, down_far, 0)))

    def hold(ahead):
        out_cut[3], ahead = tie(out_cut[3], ahead)
        return ahead

    slope_panel = spread(slope_own, -1, {4: hold})
    out_y = sum_y(*out_cut)
    up_sent = shift(dot(tok_panel[:, width:], slope_panel, 0, 0).astype(thin), "xl", 1)
    in_core = sum_core(slope_panel, up_near, up_far, 1)
    out_x = sum_x(out_y)
    down_kept = dot(act_panel, grad_panel[:, :width], 0, 0).astype(thin)
    up_kept = dot(tok_panel[:, :width], slope_panel, 0, 0).astype(thin)
    in_y = sum_y(*cut_y(in_core))
    in_x = sum_x(in_y)
    down_grad = put_half(jnp.zeros_like(down_weight), down_kept, side, 0)
    down_grad = put_half(down_grad, after(down_sent, in_core), 1 - side, 0)
    up_grad = put_half(jnp.zeros_like(up_weight), up_kept, side, 1)
    output = sum(after(out_x, in_y)).astype(thin)
    input_grad = sum(in_x).astype(thin)
    up_grad = put_half(up_grad, after(up_sent, in_y), 1 - side, 1)
    return (output, input_grad, up_grad, down_grad)


def solution(mesh):
    fine = Mesh(mesh.devices.reshape(2, 8, 4, 2, 2), ("xl", "z", "y", "xh", "core"))
    row, col = ("xl", "z"), ("y", "xh", "core")
    placed = (P(col, row), P(row, col), P(col, row), P(col, row))
    return jax.shard_map(
        local,
        mesh=fine,
        in_specs=placed,
        out_specs=(P(col, row), P(col, row), P(row, col), P(col, row)),
        check_vma=False,
    )
```

```python
import jax
import jax.numpy as jnp
from jax import lax
from jax.sharding import Mesh
from jax.sharding import PartitionSpec as P

gelu_scale = 0.7978845608028654
wide, thin = jnp.float32, jnp.bfloat16


def gelu_tanh(values):
    return (
        0.5 * values * (1.0 + jnp.tanh(gelu_scale * (values + 0.044715 * values * values * values)))
    )


def dot(left, right, left_dim, right_dim):
    return lax.dot_general(
        left, right, (((left_dim,), (right_dim,)), ((), ())), preferred_element_type=wide
    )


def shift(block, axis, by):
    size = lax.axis_size(axis)
    return lax.ppermute(block, axis, [(at, (at + by) % size) for at in range(size)])


def ring_sum(part, axis, way, hooks=None, first=None):
    half = lax.axis_size(axis) // 2
    ahead, behind = part(way * half).astype(thin) if first is None else first, None
    for step in range(1, half + 1):
        ahead = shift(ahead, axis, way)
        if hooks and step in hooks:
            ahead = hooks[step](ahead)
        ahead = ahead.astype(wide)
        if step > 1:
            behind = shift(behind, axis, -way).astype(wide)
        if step < half:
            ahead = (part(way * (half - step)) + ahead).astype(thin)
            term = part(-way * (half - step))
            behind = (term if behind is None else term + behind).astype(thin)
    return part(0) + ahead + behind


def ring_spread(block, axis, way, put, hooks=None):
    half = lax.axis_size(axis) // 2
    put(0, block)
    ahead = behind = block
    for step in range(1, half + 1):
        if hooks and step in hooks:
            ahead = hooks[step](ahead)
        ahead = shift(ahead, axis, way)
        put(-way * step, ahead)
        if step < half:
            behind = shift(behind, axis, -way)
            put(way * step, behind)


def send_to(block, axes, where):
    sizes = [lax.axis_size(axis) for axis in axes]
    total = 1
    for size in sizes:
        total *= size

    def target(at):
        spots, rest = [], at
        for size in reversed(sizes):
            spots.append(rest % size)
            rest //= size
        index = 0
        for spot, size, by in zip(reversed(spots), sizes, where):
            index = index * size + (spot + by) % size
        return index

    return lax.ppermute(block, axes, [(at, target(at)) for at in range(total)])


def gather_first(block):
    side = shift(block, "xl", 1)
    below = shift(block, "xh", 1)
    corner = send_to(block, ("xl", "xh"), (1, 1))
    return jnp.concatenate(
        [
            jnp.concatenate([block, side], axis=1),
            jnp.concatenate([below, corner], axis=1),
        ],
        axis=0,
    )


def gather_y(block):
    return [block, shift(block, "y", -1), shift(block, "y", 1), shift(block, "y", 2)]


def gather_core(blocks):
    block = jnp.concatenate(blocks, axis=0)
    return jnp.concatenate([block, shift(block, "core", 1)], axis=0)


def tie(*values):
    return lax.optimization_barrier(values)


def after(value, *others):
    return lax.optimization_barrier((value, *others))[0]


def sum_core(rows, near, far, near_dim):
    half = rows.shape[0] // 2
    other, own = rows[half:], rows[:half]
    far_got = shift(dot(other, far, 1, near_dim), "core", 1)
    near_got = shift(dot(other, near, 1, near_dim), "core", 1)
    far_sum = dot(own, far, 1, near_dim) + far_got
    near_sum = dot(own, near, 1, near_dim) + near_got
    return jnp.concatenate([near_sum, far_sum], axis=1)


def cut_y(total):
    mine, following, before, across = jnp.split(total, 4, axis=0)
    return mine, following.astype(thin), before.astype(thin), across.astype(thin)


def sum_y(mine, following, before, across):
    return (
        mine
        + shift(following, "y", 1).astype(wide)
        + shift(before, "y", -1).astype(wide)
        + shift(across, "y", 2).astype(wide)
    )


def chain_y(mine, following, before, across):
    following = following + shift(across, "y", 1).astype(wide)
    return (
        mine
        + shift(following.astype(thin), "y", 1).astype(wide)
        + shift(before, "y", -1).astype(wide)
    )


def sum_x(mine):
    rows, columns = mine.shape[0] // 2, mine.shape[1] // 2
    return (
        shift(mine[:rows, columns:], "xl", 1),
        shift(mine[rows:, :columns], "xh", 1),
        send_to(mine[rows:, columns:], ("xl", "xh"), (1, 1)),
        mine[:rows, :columns],
    )


def local(tokens, up_weight, down_weight, output_grad):
    width = tokens.shape[1]
    part_width = up_weight.shape[1] // 2
    spots = lax.axis_size("z")
    here, side = lax.axis_index("z"), lax.axis_index("xl")

    def up_cut(which):
        return lax.dynamic_slice_in_dim(up_weight, which * part_width, part_width, 1)

    def down_cut(which):
        return lax.dynamic_slice_in_dim(down_weight, which * part_width, part_width, 0)

    both = gather_first(jnp.concatenate([tokens, output_grad], axis=0))
    both = both.reshape(2, 2, tokens.shape[0], 2 * width)
    tok_first = both[:, 0].reshape(-1, 2 * width)
    grad_first = both[:, 1].reshape(-1, 2 * width)
    up_sent, tok_first = tie(up_cut(1 - side), tok_first)
    up_far = shift(up_sent, "xl", 1)
    tok_blocks = gather_y(tok_first)
    up_far, *tok_blocks = tie(up_far, *tok_blocks)
    down_cut_far, up_far = tie(down_cut(1 - side), up_far)
    down_far = shift(down_cut_far, "xl", 1)
    tok_panel = gather_core(tok_blocks)
    grad_blocks = gather_y(after(grad_first, *tok_blocks))
    up_near, down_near = up_cut(side), down_cut(side)
    count = tok_panel.shape[0]
    share = count // spots

    pre_near = dot(tok_panel[:, :width], up_near, 1, 0)
    pre_part = pre_near + dot(tok_panel[:, width:], up_far, 1, 0)
    def rows_of(panel, away):
        return lax.dynamic_slice_in_dim(panel, (here + away) % spots * share, share, 0)

    held = {}

    def hold_grad(ahead):
        grad_here = jnp.concatenate(grad_blocks, axis=0)
        ahead, held["down_far"], grad_there = tie(ahead, down_far, shift(grad_here, "core", 1))
        held["panel"] = jnp.concatenate([grad_here, grad_there], axis=0)
        near = dot(held["panel"][:, :width], down_near, 1, 1)
        held["part"] = near + dot(held["panel"][:, width:], held["down_far"], 1, 1)
        return ahead

    def hold_first(ahead):
        first = rows_of(held["part"], -spots // 2).astype(thin)
        held["first"], ahead = tie(first, ahead)
        return ahead

    pre_own = ring_sum(
        lambda away: rows_of(pre_part, away), "z", 1, {1: hold_grad, 2: hold_first}
    )
    down_far, grad_panel, grad_part = held["down_far"], held["panel"], held["part"]
    grad_own = ring_sum(
        lambda away: rows_of(grad_part, away), "z", -1, None, held["first"]
    )

    activ_own, pullback = jax.vjp(gelu_tanh, pre_own)
    activ_own = activ_own.astype(thin)
    slope_own = pullback(grad_own)[0].astype(thin)

    def spread(block, way, hooks=None):
        panel = [jnp.zeros((count, part_width), thin)]

        def put(away, value):
            panel[0] = lax.dynamic_update_slice_in_dim(
                panel[0], value, (here + away) % spots * share, 0
            )

        ring_spread(block, "z", way, put, hooks)
        return panel[0]

    def put_half(whole, value, which, axis):
        return lax.dynamic_update_slice_in_dim(whole, value, which * part_width, axis)

    act_panel = spread(activ_own, 1)
    down_prod = dot(act_panel, grad_panel[:, width:], 0, 0).astype(thin)
    down_first, down_last = jnp.split(down_prod, 2, axis=0)
    down_first = shift(down_first, "xl", 1)
    down_last, down_first = tie(down_last, down_first)
    down_last = shift(down_last, "xl", 1)
    out_core = sum_core(act_panel, down_near, down_far, 0)
    out_cut = list(cut_y(out_core))
    out_cut[1] = jnp.split(out_core, 4, axis=0)[1]

    def hold(ahead):
        out_cut[3], ahead = tie(out_cut[3], ahead)
        return ahead

    slope_panel = spread(slope_own, -1, {4: hold})
    out_y = chain_y(*out_cut)
    up_sent = shift(dot(tok_panel[:, width:], slope_panel, 0, 0).astype(thin), "xl", 1)
    in_core = sum_core(slope_panel, up_near, up_far, 1)
    out_x = sum_x(out_y)
    down_kept = dot(act_panel, grad_panel[:, :width], 0, 0).astype(thin)
    up_kept = dot(tok_panel[:, :width], slope_panel, 0, 0).astype(thin)
    in_cut = list(cut_y(in_core))
    down_last, in_cut[3] = tie(down_last, in_cut[3])
    down_sent = jnp.concatenate([down_first, down_last], axis=0)
    in_y = sum_y(*in_cut)
    in_x = sum_x(in_y)
    down_grad = put_half(jnp.zeros_like(down_weight), down_kept, side, 0)
    down_grad = put_half(down_grad, down_sent, 1 - side, 0)
    up_grad = put_half(jnp.zeros_like(up_weight), up_kept, side, 1)
    output = sum(after(out_x, in_y)).astype(thin)
    input_grad = sum(in_x).astype(thin)
    up_grad = put_half(up_grad, after(up_sent, in_y), 1 - side, 1)
    return (output, input_grad, up_grad, down_grad)


def solution(mesh):
    fine = Mesh(mesh.devices.reshape(2, 8, 4, 2, 2), ("xl", "z", "y", "xh", "core"))
    row, col = ("xl", "z"), ("y", "xh", "core")
    placed = (P(col, row), P(row, col), P(col, row), P(col, row))
    return jax.shard_map(
        local,
        mesh=fine,
        in_specs=placed,
        out_specs=(P(col, row), P(col, row), P(row, col), P(col, row)),
        check_vma=False,
    )
```

```python
import jax
import jax.numpy as jnp
from jax import lax
from jax.sharding import Mesh
from jax.sharding import PartitionSpec as P

gelu_scale = 0.7978845608028654
wide, thin = jnp.float32, jnp.bfloat16


def gelu_tanh(values):
    return (
        0.5 * values * (1.0 + jnp.tanh(gelu_scale * (values + 0.044715 * values * values * values)))
    )


def dot(left, right, left_dim, right_dim):
    return lax.dot_general(
        left, right, (((left_dim,), (right_dim,)), ((), ())), preferred_element_type=wide
    )


def shift(block, axis, by):
    size = lax.axis_size(axis)
    return lax.ppermute(block, axis, [(at, (at + by) % size) for at in range(size)])


def ring_sum(part, axis, way, hooks=None, first=None):
    half = lax.axis_size(axis) // 2
    ahead, behind = part(way * half).astype(thin) if first is None else first, None
    for step in range(1, half + 1):
        ahead = shift(ahead, axis, way)
        if hooks and step in hooks:
            ahead = hooks[step](ahead)
        ahead = ahead.astype(wide)
        if step > 1:
            behind = shift(behind, axis, -way).astype(wide)
        if step < half:
            ahead = (part(way * (half - step)) + ahead).astype(thin)
            term = part(-way * (half - step))
            behind = (term if behind is None else term + behind).astype(thin)
    return part(0) + ahead + behind


def ring_spread(block, axis, way, put, hooks=None):
    half = lax.axis_size(axis) // 2
    put(0, block)
    ahead = behind = block
    for step in range(1, half + 1):
        if hooks and step in hooks:
            ahead = hooks[step](ahead)
        ahead = shift(ahead, axis, way)
        put(-way * step, ahead)
        if step < half:
            behind = shift(behind, axis, -way)
            put(way * step, behind)


def send_to(block, axes, where):
    sizes = [lax.axis_size(axis) for axis in axes]
    total = 1
    for size in sizes:
        total *= size

    def target(at):
        spots, rest = [], at
        for size in reversed(sizes):
            spots.append(rest % size)
            rest //= size
        index = 0
        for spot, size, by in zip(reversed(spots), sizes, where):
            index = index * size + (spot + by) % size
        return index

    return lax.ppermute(block, axes, [(at, target(at)) for at in range(total)])


def gather_first(block):
    side = shift(block, "xl", 1)
    below = shift(block, "xh", 1)
    corner = send_to(block, ("xl", "xh"), (1, 1))
    return jnp.concatenate(
        [
            jnp.concatenate([block, side], axis=1),
            jnp.concatenate([below, corner], axis=1),
        ],
        axis=0,
    )


def gather_y(block):
    return [block, shift(block, "y", -1), shift(block, "y", 1), shift(block, "y", 2)]


def gather_core(blocks):
    block = jnp.concatenate(blocks, axis=0)
    return jnp.concatenate([block, shift(block, "core", 1)], axis=0)


def tie(*values):
    return lax.optimization_barrier(values)


def after(value, *others):
    return lax.optimization_barrier((value, *others))[0]


def sum_core(rows, near, far, near_dim):
    half = rows.shape[0] // 2
    other, own = rows[half:], rows[:half]
    far_got = shift(dot(other, far, 1, near_dim), "core", 1)
    near_got = shift(dot(other, near, 1, near_dim), "core", 1)
    far_sum = dot(own, far, 1, near_dim) + far_got
    near_sum = dot(own, near, 1, near_dim) + near_got
    return jnp.concatenate([near_sum, far_sum], axis=1)


def cut_y(total):
    mine, following, before, across = jnp.split(total, 4, axis=0)
    return mine, following.astype(thin), before.astype(thin), across.astype(thin)


def sum_y(mine, following, before, across):
    return (
        mine
        + shift(following, "y", 1).astype(wide)
        + shift(before, "y", -1).astype(wide)
        + shift(across, "y", 2).astype(wide)
    )


def chain_y(mine, following, before, across):
    following = following + shift(across, "y", 1).astype(wide)
    return (
        mine
        + shift(following.astype(thin), "y", 1).astype(wide)
        + shift(before, "y", -1).astype(wide)
    )


def sum_x(mine):
    rows, columns = mine.shape[0] // 2, mine.shape[1] // 2
    return (
        shift(mine[:rows, columns:], "xl", 1),
        shift(mine[rows:, :columns], "xh", 1),
        send_to(mine[rows:, columns:], ("xl", "xh"), (1, 1)),
        mine[:rows, :columns],
    )


def local(tokens, up_weight, down_weight, output_grad):
    width = tokens.shape[1]
    part_width = up_weight.shape[1] // 2
    spots = lax.axis_size("z")
    here, side = lax.axis_index("z"), lax.axis_index("xl")

    def up_cut(which):
        return lax.dynamic_slice_in_dim(up_weight, which * part_width, part_width, 1)

    def down_cut(which):
        return lax.dynamic_slice_in_dim(down_weight, which * part_width, part_width, 0)

    both = gather_first(jnp.concatenate([tokens, output_grad], axis=0))
    both = both.reshape(2, 2, tokens.shape[0], 2 * width)
    tok_first = both[:, 0].reshape(-1, 2 * width)
    grad_first = both[:, 1].reshape(-1, 2 * width)
    up_sent, tok_first = tie(up_cut(1 - side), tok_first)
    up_far = shift(up_sent, "xl", 1)
    tok_blocks = gather_y(tok_first)
    up_far, *tok_blocks = tie(up_far, *tok_blocks)
    down_cut_far, up_far = tie(down_cut(1 - side), up_far)
    down_far = shift(down_cut_far, "xl", 1)
    tok_panel = gather_core(tok_blocks)
    grad_blocks = gather_y(after(grad_first, *tok_blocks))
    up_near, down_near = up_cut(side), down_cut(side)
    count = tok_panel.shape[0]
    share = count // spots

    pre_near = dot(tok_panel[:, :width], up_near, 1, 0)
    pre_part = pre_near + dot(tok_panel[:, width:], up_far, 1, 0)
    def rows_of(panel, away):
        return lax.dynamic_slice_in_dim(panel, (here + away) % spots * share, share, 0)

    held = {}

    def hold_grad(ahead):
        grad_here = jnp.concatenate(grad_blocks, axis=0)
        ahead, held["down_far"], grad_there = tie(ahead, down_far, shift(grad_here, "core", 1))
        held["panel"] = jnp.concatenate([grad_here, grad_there], axis=0)
        near = dot(held["panel"][:, :width], down_near, 1, 1)
        held["part"] = near + dot(held["panel"][:, width:], held["down_far"], 1, 1)
        return ahead

    def hold_first(ahead):
        first = rows_of(held["part"], -spots // 2).astype(thin)
        held["first"], ahead = tie(first, ahead)
        return ahead

    pre_own = ring_sum(
        lambda away: rows_of(pre_part, away), "z", 1, {1: hold_grad, 2: hold_first}
    )
    down_far, grad_panel, grad_part = held["down_far"], held["panel"], held["part"]
    grad_own = ring_sum(
        lambda away: rows_of(grad_part, away), "z", -1, None, held["first"]
    )

    activ_own, pullback = jax.vjp(gelu_tanh, pre_own)
    activ_own = activ_own.astype(thin)
    slope_own = pullback(grad_own)[0].astype(thin)

    def spread(block, way, hooks=None):
        panel = [jnp.zeros((count, part_width), thin)]

        def put(away, value):
            panel[0] = lax.dynamic_update_slice_in_dim(
                panel[0], value, (here + away) % spots * share, 0
            )

        ring_spread(block, "z", way, put, hooks)
        return panel[0]

    def put_half(whole, value, which, axis):
        return lax.dynamic_update_slice_in_dim(whole, value, which * part_width, axis)

    act_panel = spread(activ_own, 1)
    down_prod = dot(act_panel, grad_panel[:, width:], 0, 0).astype(thin)
    down_first, down_last = jnp.split(down_prod, 2, axis=0)
    down_first = shift(down_first, "xl", 1)
    down_last, down_first = tie(down_last, down_first)
    down_last = shift(down_last, "xl", 1)
    out_core = sum_core(act_panel, down_near, down_far, 0)
    out_cut = list(cut_y(out_core))
    out_cut[1] = jnp.split(out_core, 4, axis=0)[1]

    def hold(ahead):
        out_cut[3], ahead = tie(out_cut[3], ahead)
        return ahead

    slope_panel = spread(slope_own, -1, {4: hold})
    out_y = chain_y(*out_cut)
    up_first, up_last = jnp.split(
        dot(tok_panel[:, width:], slope_panel, 0, 0).astype(thin), 2, axis=0
    )
    up_first = shift(up_first, "xl", 1)
    up_last, up_first = tie(up_last, up_first)
    up_last = shift(up_last, "xl", 1)
    in_core = sum_core(slope_panel, up_near, up_far, 1)
    out_x = sum_x(out_y)
    down_kept = dot(act_panel, grad_panel[:, :width], 0, 0).astype(thin)
    up_kept = dot(tok_panel[:, :width], slope_panel, 0, 0).astype(thin)
    in_cut = list(cut_y(in_core))
    down_last, in_cut[3] = tie(down_last, in_cut[3])
    down_sent = jnp.concatenate([down_first, down_last], axis=0)
    in_y = sum_y(*in_cut)
    in_x = sum_x(in_y)
    down_grad = put_half(jnp.zeros_like(down_weight), down_kept, side, 0)
    down_grad = put_half(down_grad, down_sent, 1 - side, 0)
    up_grad = put_half(jnp.zeros_like(up_weight), up_kept, side, 1)
    output = sum(after(out_x, in_y)).astype(thin)
    input_grad = sum(in_x).astype(thin)
    up_grad = put_half(up_grad, jnp.concatenate([up_first, up_last], axis=0), 1 - side, 1)
    return (output, input_grad, up_grad, down_grad)


def solution(mesh):
    fine = Mesh(mesh.devices.reshape(2, 8, 4, 2, 2), ("xl", "z", "y", "xh", "core"))
    row, col = ("xl", "z"), ("y", "xh", "core")
    placed = (P(col, row), P(row, col), P(col, row), P(col, row))
    return jax.shard_map(
        local,
        mesh=fine,
        in_specs=placed,
        out_specs=(P(col, row), P(col, row), P(row, col), P(col, row)),
        check_vma=False,
    )
```
